256 devices in a mesh: head: 8 (over x, core), ctx: 32 (over z, y).
Axes of the slice: x: 4, y: 4, z: 8, core: 2. Of those that a mesh axis runs over, the one named last changes fastest.
Arguments:
- queries: bfloat16 [32, 1024, 8192], P('ctx', 'head'), may hold values from -9 to 9
- segment_kv: bfloat16 [32, 1024, 2048], P('ctx', 'head'), may hold values from -9 to 9
- cache_kv: bfloat16 [131072, 2048], P('ctx', 'head'), may hold values from -6 to 6
- vertical_ids: int32 [8, 32, 2], P('head', 'ctx'), may hold values from 0 to 47, as said below
- vertical_counts: int32 [8, 32], P('head'), may hold values from 1 to 2, as said below
- vertical_heads: int32 [64, 64], P('head'), may hold values from 0 to 1, as said below
- slash_offsets: int32 [64, 4], P('head'), may hold values from 0 to 15, as said below
- slash_counts: int32 [64], P('head'), may hold values from 1 to 4
Outputs:
- attended: bfloat16 [32, 1024, 8192], P('ctx', 'head')
The draws below stay inside these ranges and needn't reach their ends.
Inputs may be any that keep to these rules, and one draw needn't show every extreme that they name: `vertical_ids`: block numbers within one context shard's prefix; the 2 slots of one KV head and shard hold distinct blocks. `vertical_counts`: some shard of each KV head has all 2 slots live. `vertical_heads`: marks stand only on live slots; a head marks at most 8 slots, and some head exactly 8. `slash_offsets`: slot 0 holds 0; the offsets of one head are distinct.
All inputs are finite; a program needn't handle non-finite values.
Results may differ from the reference program's by a relative error of at most 0.0043.
Values may be sent and summed in bfloat16 or wider, within the bound.
A program may use at most 128 MiB of HBM per device.

```python
import jax
import jax.numpy as jnp
from jax import lax

H = 64
KVH = 8
HEAD_WIDTH = 128
BLOCK_POSITIONS = 64
CAPU = 2
NCHUNK = 32
SHARD_LEN = 1024
PREFIX = 131072
PBLK = 64
NQB = 16
CAPS = 4
VERTICAL_LIMIT = 8


def live_counts(key):
    counts = jax.random.randint(jax.random.fold_in(key, 201), (KVH, NCHUNK), 1, CAPU + 1)
    full_at = jax.random.randint(jax.random.fold_in(key, 202), (KVH, 1), 0, NCHUNK)
    owners = jnp.arange(NCHUNK, dtype=jnp.int32)[None, :]
    return jnp.where(owners == full_at, CAPU, counts).astype(jnp.int32)


def draw_queries(key, part):
    key = jax.random.fold_in(key, 1)
    return jax.random.truncated_normal(key, -6.0, 6.0, (NCHUNK, SHARD_LEN, H * HEAD_WIDTH), jnp.float32).astype(jnp.bfloat16)


def draw_segment_kv(key, part):
    key = jax.random.fold_in(key, 2)
    return jax.random.truncated_normal(key, -6.0, 6.0, (NCHUNK, SHARD_LEN, KVH * 2 * HEAD_WIDTH), jnp.float32).astype(jnp.bfloat16)


def draw_vertical_ids(key, part):
    key = jax.random.fold_in(key, 3)
    span_size = (PBLK - NQB) // CAPU
    slot_ids = jnp.arange(CAPU, dtype=jnp.int32)[None, None, :]
    block_ids = slot_ids * span_size + jax.random.randint(key, (KVH, NCHUNK, CAPU), 0, span_size)
    corner = (jnp.arange(KVH)[:, None, None] == 0) & (jnp.arange(NCHUNK)[None, :, None] == 0) & (slot_ids == CAPU - 1)
    return jnp.where(corner, CAPU * span_size - 1, block_ids).astype(jnp.int32)


def draw_vertical_counts(key, part):
    counts = live_counts(key)
    return counts


def draw_vertical_heads(key, part):
    counts = live_counts(key)
    key = jax.random.fold_in(key, 5)
    columns = NCHUNK * CAPU
    slot_ids = jnp.arange(CAPU, dtype=jnp.int32)
    live_slots = (slot_ids[None, None, :] < counts[:, :, None]).reshape(KVH, columns)
    live_heads = jnp.repeat(live_slots, H // KVH, axis=0)
    head_keys = jax.random.split(key, H + 2)
    shuffled = jax.vmap(lambda sub_key: jax.random.permutation(sub_key, columns))(head_keys[:H])
    priority = jnp.where(live_heads, 0, columns) + shuffled
    ranking = jnp.argsort(jnp.argsort(priority, axis=1, stable=True), axis=1, stable=True)
    crowded_heads = jax.random.randint(head_keys[H], (H,), 0, 4) == 0
    forced = jax.random.randint(head_keys[H + 1], (), 0, H)
    crowded_heads = crowded_heads | (jnp.arange(H) == forced)
    block_allowance = jnp.where(crowded_heads, VERTICAL_LIMIT, max(1, VERTICAL_LIMIT // 10))
    return (ranking < block_allowance[:, None]).astype(jnp.int32)


def draw_slash_offsets(key, part):
    key = jax.random.fold_in(key, 6)
    head_keys = jax.random.split(key, H + 1)
    shuffled = jax.vmap(lambda sub_key: jax.random.permutation(sub_key, NQB - 1))(head_keys[:H])
    rolled = (shuffled - shuffled[:, :1] + NQB - 2) % (NQB - 1)
    forced = jax.random.randint(head_keys[H], (), 0, H)
    shuffled = jnp.where((jnp.arange(H) == forced)[:, None], rolled, shuffled)
    chosen = shuffled[:, :CAPS - 1] + 1
    return jnp.concatenate([jnp.zeros((H, 1), jnp.int32), chosen.astype(jnp.int32)], axis=1)


def draw_slash_counts(key, part):
    key = jax.random.fold_in(key, 7)
    counts = jax.random.randint(key, (H,), 1, CAPS + 1)
    forced = jax.random.randint(jax.random.fold_in(key, 1), (), 0, H)
    return jnp.where(jnp.arange(H) == forced, CAPS, counts).astype(jnp.int32)


def steps_of(key, shape, shards, smallest, high):
    loudness = 1.0
    for dim, blocks in shards:
        draws = jax.random.uniform(jax.random.fold_in(jax.random.fold_in(key, 6), dim), (blocks,), jnp.float32, smallest / len(shards), high / len(shards))
        loudness = loudness * jnp.repeat(jnp.exp(draws), shape[dim] // blocks).reshape((-1,) + (1,) * (len(shape) - 1 - dim))
    return loudness


def gaussian(key, shape, scale, reach, pieces=(), kind=jnp.bfloat16):
    drawn = scale * jax.random.normal(key, shape, jnp.float32)
    if pieces:
        drawn = drawn * steps_of(key, shape, pieces, -0.22, 0.18)
    return jnp.clip(drawn, -reach, reach).astype(kind)


def setup_inputs(seed: int = 0) -> dict:
    seeds = jax.random.split(jax.random.key(seed), 9)
    return {
        "queries": draw_queries(jax.random.fold_in(seeds[8], 71), 0),
        "segment_kv": draw_segment_kv(jax.random.fold_in(seeds[8], 71), 0),
        "cache_kv": gaussian(seeds[2], (PREFIX, KVH * 2 * HEAD_WIDTH), 1.0, 6.0, ((0, 32), (1, 8))),
        "vertical_ids": draw_vertical_ids(jax.random.fold_in(seeds[8], 71), 0),
        "vertical_counts": draw_vertical_counts(jax.random.fold_in(seeds[8], 71), 0),
        "vertical_heads": draw_vertical_heads(jax.random.fold_in(seeds[8], 71), 0),
        "slash_offsets": draw_slash_offsets(jax.random.fold_in(seeds[8], 71), 0),
        "slash_counts": draw_slash_counts(jax.random.fold_in(seeds[8], 71), 0),
    }


NEG_FILL = -1.0e30


def reference(queries, segment_kv, cache_kv, vertical_ids, vertical_counts, vertical_heads, slash_offsets, slash_counts):
    seg_len = NCHUNK * SHARD_LEN
    seg_blocks = seg_len // BLOCK_POSITIONS
    prefix_blocks = NCHUNK * PBLK
    group_size = H // KVH
    score_scale = HEAD_WIDTH ** -0.5
    head_rows = queries.reshape(seg_len, H, HEAD_WIDTH).transpose(1, 0, 2)
    full_kv = jnp.concatenate([cache_kv.reshape(PREFIX, KVH, 2 * HEAD_WIDTH), segment_kv.reshape(seg_len, KVH, 2 * HEAD_WIDTH)], axis=0)
    full_blocks = full_kv.reshape(prefix_blocks + seg_blocks, BLOCK_POSITIONS, KVH, 2 * HEAD_WIDTH)
    columns = NCHUNK * CAPU
    slot_ids = jnp.arange(CAPU, dtype=jnp.int32)
    owners = jnp.arange(NCHUNK, dtype=jnp.int32)
    live_slots = (slot_ids[None, None, :] < vertical_counts[:, :, None]).reshape(KVH, columns)
    global_ids = (owners[None, :, None] * PBLK + vertical_ids).reshape(KVH, columns).astype(jnp.int32)
    positions = jnp.arange(BLOCK_POSITIONS, dtype=jnp.int32)
    causal = positions[None, :] <= positions[:, None]
    block_ids = jnp.arange(seg_blocks, dtype=jnp.int32)

    def one_head(inputs):
        rows_in, member, offsets, slash_count, head_index = inputs
        kv_pick = head_index // group_size
        head_blocks = jnp.take(full_blocks, kv_pick, axis=2)
        flagged_blocks = (member == 1) & jnp.take(live_slots, kv_pick, axis=0)
        sorted_order = jnp.argsort(jnp.where(flagged_blocks, 0, 1), stable=True)[:VERTICAL_LIMIT]
        vert_keep = jnp.repeat(flagged_blocks[sorted_order], BLOCK_POSITIONS)[None, :]
        column_key_value = head_blocks[jnp.take(global_ids, kv_pick, axis=0)[sorted_order]]
        column_key_rows = column_key_value[:, :, :HEAD_WIDTH].reshape(VERTICAL_LIMIT * BLOCK_POSITIONS, HEAD_WIDTH)
        column_value_rows = column_key_value[:, :, HEAD_WIDTH:].reshape(VERTICAL_LIMIT * BLOCK_POSITIONS, HEAD_WIDTH)
        vert_scores = jnp.dot(rows_in, column_key_rows.T, preferred_element_type=jnp.float32) * score_scale
        key_blocks = (prefix_blocks + block_ids[:, None] - offsets[None, :]).astype(jnp.int32)
        slash_kv = head_blocks[key_blocks]
        q_blocks = rows_in.reshape(seg_blocks, BLOCK_POSITIONS, HEAD_WIDTH).astype(jnp.float32)
        slash_scores = jnp.einsum("gqd,gskd->gqsk", q_blocks, slash_kv[..., :HEAD_WIDTH].astype(jnp.float32)) * score_scale
        slash_live = jnp.arange(CAPS, dtype=jnp.int32) < slash_count
        slash_keep = slash_live[None, None, :, None] & ((offsets > 0)[None, None, :, None] | causal[None, :, None, :])
        vert_max = jnp.max(jnp.where(vert_keep, vert_scores, NEG_FILL), axis=1)
        slash_max = jnp.max(jnp.where(slash_keep, slash_scores, NEG_FILL), axis=(2, 3)).reshape(seg_len)
        row_max = jnp.maximum(vert_max, slash_max)
        vert_weights = jnp.where(vert_keep, jnp.exp(vert_scores - row_max[:, None]), 0.0)
        slash_weights = jnp.where(slash_keep, jnp.exp(slash_scores - row_max.reshape(seg_blocks, BLOCK_POSITIONS)[:, :, None, None]), 0.0)
        row_total = jnp.sum(vert_weights, axis=1) + jnp.sum(slash_weights, axis=(2, 3)).reshape(seg_len)
        vert_rounded = vert_weights.astype(jnp.bfloat16)
        slash_rounded = lax.optimization_barrier(slash_weights.astype(jnp.bfloat16))
        summed = jnp.dot(vert_rounded, column_value_rows, preferred_element_type=jnp.float32)
        summed = summed + jnp.einsum("gqsk,gskd->gqd", slash_rounded.astype(jnp.float32), slash_kv[..., HEAD_WIDTH:].astype(jnp.float32)).reshape(seg_len, HEAD_WIDTH)
        return (summed / row_total[:, None]).astype(jnp.bfloat16)

    attended = lax.map(one_head, (head_rows, vertical_heads, slash_offsets, slash_counts, jnp.arange(H, dtype=jnp.int32)))
    return attended.transpose(1, 0, 2).reshape(NCHUNK, SHARD_LEN, H * HEAD_WIDTH)
```

```python
import functools
import math

import jax
import jax.numpy as jnp
from jax import lax
from jax.experimental import pallas as pl
from jax.experimental.pallas import tpu as pltpu
from jax.sharding import PartitionSpec as P

MESH = pl.DeviceIdType.MESH
W = 128
BLK = 64
CH = 128
TAIL = 960
NEG = -1e30
COEF = W**-0.5 * math.log2(math.e)


def kernel(
    ids_ref,
    counts_ref,
    offs_ref,
    slash_ref,
    heads_ref,
    q_ref,
    kv_ref,
    cache_ref,
    out_ref,
    qin,
    obuf,
    band0,
    band1,
    pool0,
    pool1,
    cachev,
    vg,
    par,
    lst,
    lists,
    loc,
    k0s,
    k0r,
    k1s,
    k1r,
    cs,
    qs,
    qr,
    os_,
    or_,
    ts,
    tr,
    xs,
    xr,
    ps,
    pr,
):
    h = lax.axis_index("head")
    c = lax.axis_index("ctx")
    x, core = h // 2, lax.rem(h, 2)
    z, y = c // 4, lax.rem(c, 4)
    far = lax.rem(h + 4, 8)
    D = 1 - 2 * core
    mate = x * 2 + 1 - core
    mate_far = lax.rem(mate + 4, 8)
    nxt = lax.rem(c + 1, 32)
    prv = lax.rem(c + 31, 32)

    def hx(d, cc):
        return hs[d, cc]

    zs = {s: lax.rem(z + s * D + 16, 8) for s in range(-4, 4)}
    ys = {s: lax.rem(y + s * D + 8, 4) for s in range(-2, 3)}
    hs = {(d, cc): lax.rem(x + d + 4, 4) * 2 + cc for d in (-1, 1) for cc in (0, 1)}

    def zz(s):
        return zs[s]

    def yy(s):
        return ys[s]

    def zdev(s):
        return (h, zz(s) * 4 + y)

    def ydev(s):
        return (h, z * 4 + yy(s))

    sent = []
    band, pool = (band0, band1), (pool0, pool1)

    def go(make, cond=None):
        if cond is None:
            make().start()
        else:

            @pl.when(cond())
            def _():
                make().start()

        sent.append((make, cond))

    def remote(src, dst, ss, rs, dev):
        return pltpu.make_async_remote_copy(
            src_ref=src, dst_ref=dst, send_sem=ss, recv_sem=rs, device_id=dev, device_id_type=MESH
        )

    def arrived(dst, ss, rs):
        remote(dst, dst, ss, rs, (h, c)).wait_recv()

    def head_cols(ref, j, width):
        return ref.at[0, :, pl.ds(pl.multiple_of(j * width, width), width)]

    def kv_cols(j):
        return kv_ref.at[:, :, pl.ds(pl.multiple_of(j * 256, 256), 256)]

    def rows_of(s, start, size=CH):
        return band[s].at[pl.ds(start // BLK, size // BLK)]

    load_cache = pltpu.make_async_copy(cache_ref.at[pl.ds(0, 48)], cachev, loc.at[0])
    load_cache.start()
    locals_ = [
        pltpu.make_async_copy(src, dst, loc.at[2 + i])
        for i, (src, dst) in enumerate(
            [
                (kv_cols(h), rows_of(0, TAIL + CH * h)),
                (kv_cols(far), rows_of(1, 1024 + CH * core)),
                (head_cols(q_ref, h, 1024), qin.at[4 + core]),
                (head_cols(q_ref, far, 1024), qin.at[6 + core]),
            ]
        )
    ]
    for cp in locals_:
        cp.start()

    barrier = pltpu.get_barrier_semaphore()

    def greet(dev):
        pl.semaphore_signal(barrier, inc=1, device_id=dev, device_id_type=MESH)

    for s in (-2, -1, 1, 2):
        greet(zdev(s))
    for s in (-1, 1, 2):
        greet(ydev(s))

    @pl.when(c > 0)
    def _():
        for r in range(8):
            greet((r, prv))

    @pl.when(c == 0)
    def _():
        greet((h, 31))
        greet((far, 31))

    for r in range(1, 8):
        greet((lax.rem(h + r, 8), c))

    lane = lax.broadcasted_iota(jnp.int32, (8, 128), 1)
    row = lax.broadcasted_iota(jnp.int32, (8, 128), 0)
    live = jnp.zeros((8, 128), jnp.int32)
    for i in range(32):
        live = jnp.where(lane // 2 == i, counts_ref[0, i], live)
    table = jnp.zeros((8, 128), jnp.int32)
    for j in range(8):
        for i in range(4):
            table = jnp.where((row == j) & (lane == 64 + i), offs_ref[i, j], table)
        table = jnp.where((row == j) & (lane == 68), slash_ref[0, j], table)
    par[0] = table
    par[0, :, 0:64] = jnp.where(lax.rem(lane, 2) < live, 1, 0)[:, 0:64] * heads_ref[...]

    @pl.when(c < 31)
    def _():
        pl.semaphore_wait(barrier, 22)

    @pl.when(c == 31)
    def _():
        pl.semaphore_wait(barrier, 16)

    def piece(k, zpos, ypos):
        return pool[k].at[pl.ds((zpos * 4 + ypos) * 2, 2)]

    load_cache.wait()
    for i in range(2):
        pool0[c * 2 + i] = cachev[ids_ref[0, 0, i]]

    def psend(n, place, to):
        go(lambda: remote(piece(*place()), piece(*place()), ps.at[n], pr.at[n], to()))

    def parrive(n, place):
        arrived(piece(*place()), ps.at[n], pr.at[n])

    Z, YL, YS, YF = 0, 8, 16, 24
    KX, KL, KS, KF, KZ = 32, 33, 34, 35, 36
    zorder = [0, -1, 1, -2, 2, -3, 3, -4]
    yorder = [0, -1, 1, -2]

    def k1_push(n):
        ref = lambda: (0, zz(zorder[n]), y)
        psend(YL + n, ref, lambda: ydev(1))
        psend(YS + n, ref, lambda: ydev(-1))

    def k1_arrive(n):
        ref = lambda: (0, zz(zorder[n]), y)
        parrive(Z + n, ref)
        if n == 3:
            psend(Z + 5, ref, lambda: zdev(1))
            psend(Z + 7, ref, lambda: zdev(2))
        if n == 4:
            psend(Z + 6, ref, lambda: zdev(-1))
        k1_push(n)

    def k1_forward(n):
        ref = lambda: (0, zz(zorder[n]), yy(-1))
        parrive(YL + n, ref)
        psend(YF + n, ref, lambda: ydev(1))

    def k2_zstart(n):
        ref = lambda: (1, z, yy(yorder[n]))
        psend(KZ + n, ref, lambda: zdev(1))
        psend(KZ + 16 + n, ref, lambda: zdev(-1))

    def k2_long(s, n):
        ref = lambda: (1, zz(-s), yy(yorder[n]))
        parrive(KZ + 4 * (s - 1) + n, ref)
        if s < 4:
            psend(KZ + 4 * s + n, ref, lambda: zdev(1))

    def k2_short(s, n):
        ref = lambda: (1, zz(s), yy(yorder[n]))
        parrive(KZ + 16 + 4 * (s - 1) + n, ref)
        if s < 3:
            psend(KZ + 16 + 4 * s + n, ref, lambda: zdev(-1))

    own = lambda: (0, z, y)
    for n, d in ((3, 2), (4, -2), (1, 1), (2, -1)):
        psend(Z + n, own, lambda d=d: zdev(d))
    k1_push(0)

    for r in (4, 2, 3, 5, 6, 1, 7):
        hd = lax.rem(h + r, 8)
        go(
            lambda r=r, hd=hd: remote(
                kv_cols(hd), rows_of(0, TAIL + CH * h), k0s.at[r], k0r.at[h], (hd, c)
            )
        )
    go(lambda: remote(piece(0, z, y), piece(1, z, y), ps.at[KX], pr.at[KX], (far, c)))
    go(lambda: remote(par.at[0], par.at[1], xs.at[0], xr.at[0], (far, c)))

    for d in (1, -1):
        for cc in (0, 1):
            u = (0 if d == 1 else 2) + core
            n = (0 if d == 1 else 2) + cc
            hd = hx(d, cc)
            go(
                lambda u=u, n=n, hd=hd: remote(
                    head_cols(q_ref, hd, 1024), qin.at[u], qs.at[n], qr.at[u], (hd, c)
                )
            )
    go(lambda: remote(head_cols(q_ref, mate, 1024), qin.at[4 + core], qs.at[4], qr.at[4], (mate, c)))
    go(lambda: remote(head_cols(q_ref, mate_far, 1024), qin.at[6 + core], qs.at[5], qr.at[5], (mate, c)))

    for i in range(5):
        xd = lax.rem(x + i, 4)
        cd = lax.rem(c + (x + i) // 4, 32)
        for cc in range(1 if i == 0 else 2):
            hd = mate if i == 0 else xd * 2 + cc
            n = 2 * i + cc
            across = lax.rem(hd + 4, 8)
            go(
                lambda i=i, n=n, hd=hd, cd=cd, across=across: remote(
                    kv_cols(across),
                    rows_of(1, (4 - i) * 256 + CH * core),
                    k1s.at[n],
                    k1r.at[2 * i + core],
                    (hd, cd),
                ),
                None if i == 0 else (lambda i=i: 4 * c + x + i < 128),
            )
    xfar = lax.rem(x + 2, 4)
    for i in range(1, 5):
        back = 64 - 4 * lax.max(i - xfar, 1)
        for cc in range(2):
            go(
                lambda i=i, cc=cc, back=back: remote(
                    cache_ref.at[pl.ds(back + 2 * cc, 2)],
                    rows_of(1, (4 - i) * 256 + CH * cc),
                    cs.at[2 * i + cc],
                    k1r.at[2 * i + cc],
                    (far, 0),
                ),
                lambda i=i: (c == 31) & (i > xfar),
            )

    def make_lists(s):
        rowv = par[s]
        flag = jnp.where(lane < 64, rowv, 0)
        rank = flag
        for step in (1, 2, 4, 8, 16, 32):
            rank = rank + jnp.where(lane >= step, pltpu.roll(rank, step, 1), 0)
        tab = jnp.where(lane >= 64, rowv, 0)
        for i in range(8):
            at = jnp.sum(jnp.where((flag == 1) & (rank == i + 1), lane, 0), axis=1, keepdims=True)
            tab = tab + jnp.where(lane == i, at, 0)
        tab = tab + jnp.where(lane == 8, jnp.sum(flag, axis=1, keepdims=True), 0)
        lst[s] = tab

    make_lists(0)

    @pl.loop(0, 8)
    def _(j):
        vg[j, :, 256:384] = jnp.ones((512, 128), jnp.bfloat16)

    parrive(KX, lambda: (1, z, y))
    psend(KL, lambda: (1, z, y), lambda: ydev(1))
    psend(KS, lambda: (1, z, y), lambda: ydev(-1))
    psend(KF, lambda: (1, z, y), lambda: ydev(2))
    k2_zstart(0)
    k1_arrive(1)
    k1_arrive(2)
    k1_arrive(3)
    k1_arrive(4)
    k1_forward(0)
    arrived(par.at[1], xs.at[0], xr.at[0])
    make_lists(1)
    to_smem = pltpu.make_async_copy(lst, lists, loc.at[1])
    to_smem.start()
    parrive(KL, lambda: (1, z, yy(-1)))
    k2_zstart(1)
    parrive(KS, lambda: (1, z, yy(1)))
    k2_zstart(2)
    parrive(KF, lambda: (1, z, yy(-2)))
    k2_zstart(3)

    for r in range(1, 8):
        src = lax.rem(h + r, 8)
        arrived(rows_of(0, TAIL + CH * src), k0s.at[r], k0r.at[src])
    locals_[0].wait()
    go(
        lambda: remote(rows_of(0, TAIL + BLK, TAIL), rows_of(0, 0, TAIL), ts.at[0], tr.at[0], (h, nxt)),
        lambda: c != 31,
    )
    go(
        lambda: remote(
            cache_ref.at[pl.ds(49, 15)], rows_of(0, 0, TAIL), ts.at[0], tr.at[0], (h, nxt)
        ),
        lambda: c == 31,
    )

    k2_long(1, 0)
    k2_short(1, 0)
    k1_forward(1)
    k1_forward(2)
    k1_arrive(5)
    k1_arrive(6)
    k1_arrive(7)
    k1_forward(3)
    k1_forward(4)
    for n in range(1, 4):
        k2_long(1, n)
        k2_short(1, n)
    k1_forward(5)
    k1_forward(6)
    k1_forward(7)
    for n in range(4):
        k2_long(2, n)
        k2_short(2, n)
    for n in range(8):
        parrive(YS + n, lambda n=n: (0, zz(zorder[n]), yy(1)))
    for n in range(8):
        parrive(YF + n, lambda n=n: (0, zz(zorder[n]), yy(-2)))
    to_smem.wait()
    arrived(rows_of(0, 0, TAIL), ts.at[0], tr.at[0])

    def gather(s):
        @pl.loop(0, 8)
        def _(j):
            for i in range(8):
                vg[j, pl.ds(i * BLK, BLK), 0:256] = pool[s][jnp.clip(lists[s, j, i], 0, 63)]

    nt = (((1,), (1,)), ((), ()))
    f32, bf = jnp.float32, jnp.bfloat16

    def attend(p, s, first, j):
        cols = slice(j * W, (j + 1) * W)
        q = jnp.concatenate([qin[2 * p, :, cols], qin[2 * p + 1, :, cols]], axis=0)
        vlane = lax.broadcasted_iota(jnp.int32, (1, 512), 1)
        vbias = jnp.where(vlane < lists[s, j, 8] * BLK, 0.0, NEG)
        qrow = lax.broadcasted_iota(jnp.int32, (BLK, 256), 0)
        krow = lax.broadcasted_iota(jnp.int32, (BLK, 256), 1)
        keep = ((krow >= BLK) | (krow <= qrow)) & (krow < lists[s, j, 68] * BLK)
        sv = lax.dot_general(q, vg[j, :, :W], nt, preferred_element_type=f32)
        pvs, accs = [], []
        for b in range(4):
            keys = []
            for i in range(4):
                start = first + b
                if i:
                    start = start - jnp.clip(lists[s, j, 64 + i], 0, 15)
                keys.append(band[s][start])
            ks = jnp.concatenate(keys, axis=0)
            part = slice(b * BLK, (b + 1) * BLK)
            ss = lax.dot_general(q[part], ks[:, :W], nt, preferred_element_type=f32)
            tv = sv[part] * COEF + vbias
            tsl = jnp.where(keep, ss * COEF, NEG)
            m = jnp.maximum(jnp.max(tv, axis=1, keepdims=True), jnp.max(tsl, axis=1, keepdims=True))
            pvs.append(jnp.exp2(tv - m).astype(bf))
            psl = jnp.exp2(tsl - m).astype(bf)
            vs = jnp.concatenate([ks[:, W:], jnp.ones((256, W), bf)], axis=1)
            accs.append(jnp.dot(psl, vs, preferred_element_type=f32))
        acc = jnp.dot(jnp.concatenate(pvs, axis=0), vg[j, :, W:], preferred_element_type=f32)
        acc += jnp.concatenate(accs, axis=0)
        o = (acc[:, :W] / acc[:, W:]).astype(bf)
        obuf[2 * p, :, cols] = o[:CH]
        obuf[2 * p + 1, :, cols] = o[CH:]

    def out_remote(p, cc):
        d = -1 if p == 0 else 1
        return lambda: remote(
            obuf.at[2 * p + cc],
            head_cols(out_ref, h, 1024),
            os_.at[2 * p + cc],
            or_.at[(2 if d == -1 else 0) + core],
            (hx(d, cc), c),
        )

    def out_mate(p):
        return lambda: remote(
            obuf.at[2 * p + 1 - core],
            head_cols(out_ref, h if p == 2 else far, 1024),
            os_.at[2 + p],
            or_.at[2 + p],
            (mate, c),
        )

    def own_out(p):
        return pltpu.make_async_copy(
            obuf.at[2 * p + core], head_cols(out_ref, h if p == 2 else far, 1024), loc.at[p]
        )

    gather(0)
    before, after = lax.rem(x + 3, 4), lax.rem(x + 1, 4)

    @pl.loop(0, 3)
    def _(p):
        for d in range(2):

            @pl.when(p == d)
            def _(d=d):
                for u in (2 * d, 2 * d + 1):
                    arrived(qin.at[u], qs.at[u], qr.at[u])

        @pl.when(p == 2)
        def _():
            arrived(qin.at[4 + 1 - core], qs.at[4], qr.at[4])
            locals_[2].wait()

        first = 15 + 4 * jnp.where(p == 0, before, jnp.where(p == 1, after, x))
        for j in range(8):
            attend(p, 0, first, j)

        for d in range(2):

            @pl.when(p == d)
            def _(d=d):
                out_remote(d, 0)().start()
                out_remote(d, 1)().start()
                for n in (2 * d, 2 * d + 1):
                    k2_long(3, n)
                    k2_short(3, n)

        @pl.when(p == 2)
        def _():
            out_mate(2)().start()
            own_out(2).start()

    for n in range(4):
        k2_long(4, n)
    for i in range(1, 5):
        for cc in range(2):
            arrived(rows_of(1, (4 - i) * 256 + CH * cc), k1s.at[2 * i + cc], k1r.at[2 * i + cc])
    arrived(rows_of(1, 1024 + CH * (1 - core)), k1s.at[0], k1r.at[1 - core])
    locals_[1].wait()
    gather(1)
    arrived(qin.at[6 + 1 - core], qs.at[5], qr.at[5])
    locals_[3].wait()
    for j in range(8):
        attend(3, 1, 16, j)
    out_mate(3)().start()
    own_out(3).start()

    for d in (2, 3):
        own_out(d).wait()
    for n in range(4):
        k = hx(1 if n >= 2 else -1, n % 2)
        arrived(head_cols(out_ref, k, 1024), os_.at[n], or_.at[n])
    arrived(head_cols(out_ref, mate, 1024), os_.at[4], or_.at[4])
    arrived(head_cols(out_ref, mate_far, 1024), os_.at[5], or_.at[5])
    for make in (out_remote(0, 0), out_remote(0, 1), out_remote(1, 0), out_remote(1, 1), out_mate(2), out_mate(3)):
        make().wait_send()
    for make, cond in sent:
        if cond is None:
            make().wait_send()
        else:

            @pl.when(cond())
            def _(make=make):
                make().wait_send()


def finish(src, dst, sems):
    copies = [
        pltpu.make_async_copy(src.at[0, pl.ds(16 * i, 16)], dst.at[0, pl.ds(16 * i, 16)], sems.at[i])
        for i in range(8)
    ]
    for cp in copies:
        cp.start()
    for cp in copies:
        cp.wait()


def per_device(
    queries,
    segment_kv,
    cache_kv,
    vertical_ids,
    vertical_counts,
    vertical_heads,
    slash_offsets,
    slash_counts,
):
    bf = jnp.bfloat16
    dma = pltpu.SemaphoreType.DMA
    hbm = pl.BlockSpec(memory_space=pltpu.HBM)
    smem = pl.BlockSpec(memory_space=pltpu.SMEM)
    vmem = pl.BlockSpec(memory_space=pltpu.VMEM)
    shape = jax.ShapeDtypeStruct((1, CH, 8192), bf)
    result = pl.pallas_call(
        kernel,
        out_shape=shape,
        in_specs=[smem, smem, smem, smem, vmem, hbm, hbm, hbm],
        out_specs=vmem,
        scratch_shapes=[
            pltpu.VMEM((8, CH, 1024), bf),
            pltpu.VMEM((8, CH, 1024), bf),
            pltpu.VMEM((31, BLK, 256), bf),
            pltpu.VMEM((20, BLK, 256), bf),
            pltpu.VMEM((64, BLK, 256), bf),
            pltpu.VMEM((64, BLK, 256), bf),
            pltpu.VMEM((48, BLK, 256), bf),
            pltpu.VMEM((8, 512, 384), bf),
            pltpu.VMEM((2, 8, 128), jnp.int32),
            pltpu.VMEM((2, 8, 128), jnp.int32),
            pltpu.SMEM((2, 8, 128), jnp.int32),
            dma((6,)),
            dma((8,)),
            dma((8,)),
            dma((10,)),
            dma((10,)),
            dma((10,)),
            dma((6,)),
            dma((6,)),
            dma((6,)),
            dma((6,)),
            dma((1,)),
            dma((1,)),
            dma((1,)),
            dma((1,)),
            dma((64,)),
            dma((64,)),
        ],
        compiler_params=pltpu.CompilerParams(
            collective_id=0, has_side_effects=True, vmem_limit_bytes=60 << 20
        ),
        cost_estimate=pl.CostEstimate(
            flops=2 * 2 * 8 * 1024 * 768 * W, bytes_accessed=8 << 20, transcendentals=8 * 1024 * 768
        ),
    )(
        vertical_ids,
        vertical_counts,
        slash_offsets.T,
        slash_counts.reshape(1, 8),
        vertical_heads,
        queries,
        segment_kv.reshape(2, BLK, 2048),
        cache_kv.reshape(64, BLK, 256),
    )
    return pl.pallas_call(
        finish,
        out_shape=shape,
        in_specs=[pl.BlockSpec(memory_space=pl.ANY)],
        out_specs=hbm,
        scratch_shapes=[dma((8,))],
        compiler_params=pltpu.CompilerParams(vmem_limit_bytes=8 << 20),
    )(result)


def solution(mesh):
    in_specs = (
        P("ctx", "head", None),
        P("ctx", "head", None),
        P("ctx", "head"),
        P("head", "ctx", None),
        P("head", None),
        P("head", None),
        P("head", None),
        P("head"),
    )
    return jax.shard_map(
        per_device,
        mesh=mesh,
        in_specs=in_specs,
        out_specs=P("ctx", "head", None),
        check_vma=False,
    )
```

```python
import functools
import math

import jax
import jax.numpy as jnp
from jax import lax
from jax.experimental import pallas as pl
from jax.experimental.pallas import tpu as pltpu
from jax.sharding import PartitionSpec as P

MESH = pl.DeviceIdType.MESH
W = 128
BLK = 64
CH = 128
TAIL = 960
NEG = -1e30
ORDER = (2, 1, 3)
COEF = W**-0.5 * math.log2(math.e)


def kernel(
    ids_ref,
    counts_ref,
    offs_ref,
    slash_ref,
    heads_ref,
    q_ref,
    kv_ref,
    cache_ref,
    out_ref,
    qin,
    obuf,
    band0,
    pool0,
    cachev,
    vg,
    par,
    lst,
    lists,
    loc,
    k0s,
    k0r,
    qs,
    qr,
    os_,
    or_,
    ts,
    tr,
    ps,
    pr,
):
    h = lax.axis_index("head")
    c = lax.axis_index("ctx")
    x, core = h // 2, lax.rem(h, 2)
    z, y = c // 4, lax.rem(c, 4)
    D = -1
    nxt = lax.rem(c + 1, 32)
    prv = lax.rem(c + 31, 32)

    zs = {s: lax.rem(z + s * D + 16, 8) for s in range(-4, 4)}
    ys = {s: lax.rem(y + s * D + 8, 4) for s in range(-2, 3)}
    def zz(s):
        return zs[s]

    def yy(s):
        return ys[s]

    def zdev(s):
        return (h, zz(s) * 4 + y)

    def ydev(s):
        return (h, z * 4 + yy(s))

    sent = []

    def go(make, cond=None):
        if cond is None:
            make().start()
        else:

            @pl.when(cond())
            def _():
                make().start()

        sent.append((make, cond))

    def remote(src, dst, ss, rs, dev):
        return pltpu.make_async_remote_copy(
            src_ref=src, dst_ref=dst, send_sem=ss, recv_sem=rs, device_id=dev, device_id_type=MESH
        )

    def arrived(dst, ss, rs):
        remote(dst, dst, ss, rs, (h, c)).wait_recv()

    def head_cols(ref, j, width):
        return ref.at[0, :, pl.ds(pl.multiple_of(j * width, width), width)]

    def kv_cols(j):
        return kv_ref.at[:, :, pl.ds(pl.multiple_of(j * 256, 256), 256)]

    def rows_of(start, size=CH):
        return band0.at[pl.ds(start // BLK, size // BLK)]

    load_cache = pltpu.make_async_copy(cache_ref.at[pl.ds(0, 48)], cachev, loc.at[0])
    load_cache.start()
    locals_ = [
        pltpu.make_async_copy(src, dst, loc.at[2 + i])
        for i, (src, dst) in enumerate(
            [
                (kv_cols(h), rows_of(TAIL + CH * h)),
                (head_cols(q_ref, h, 1024), qin.at[h]),
            ]
        )
    ]
    for cp in locals_:
        cp.start()

    barrier = pltpu.get_barrier_semaphore()

    def greet(dev):
        pl.semaphore_signal(barrier, inc=1, device_id=dev, device_id_type=MESH)

    for s in (-2, -1, 1, 2):
        greet(zdev(s))
    for s in (-1, 1):
        greet(ydev(s))

    greet((h, prv))
    for r in range(1, 8):
        greet((lax.rem(h + r, 8), c))

    lane = lax.broadcasted_iota(jnp.int32, (8, 128), 1)
    row = lax.broadcasted_iota(jnp.int32, (8, 128), 0)
    live = jnp.zeros((8, 128), jnp.int32)
    for i in range(32):
        live = jnp.where(lane // 2 == i, counts_ref[0, i], live)
    table = jnp.zeros((8, 128), jnp.int32)
    for j in range(8):
        for i in range(4):
            table = jnp.where((row == j) & (lane == 64 + i), offs_ref[i, j], table)
        table = jnp.where((row == j) & (lane == 68), slash_ref[0, j], table)
    par[0] = table
    par[0, :, 0:64] = jnp.where(lax.rem(lane, 2) < live, 1, 0)[:, 0:64] * heads_ref[...]

    pl.semaphore_wait(barrier, 14)

    def piece(k, zpos, ypos):
        return pool0.at[pl.ds((zpos * 4 + ypos) * 2, 2)]

    load_cache.wait()
    for i in range(2):
        pool0[c * 2 + i] = cachev[ids_ref[0, 0, i]]

    def psend(n, place, to):
        go(lambda: remote(piece(*place()), piece(*place()), ps.at[n], pr.at[n], to()))

    def parrive(n, place):
        arrived(piece(*place()), ps.at[n], pr.at[n])

    Z, YL, YS, YF = 0, 8, 16, 24
    zorder = [0, -1, 1, -2, 2, -3, 3, -4]

    def k1_push(n):
        ref = lambda: (0, zz(zorder[n]), y)
        psend(YL + n, ref, lambda: ydev(1))
        psend(YS + n, ref, lambda: ydev(-1))

    def k1_arrive(n):
        ref = lambda: (0, zz(zorder[n]), y)
        parrive(Z + n, ref)
        if n == 3:
            psend(Z + 5, ref, lambda: zdev(1))
            psend(Z + 7, ref, lambda: zdev(2))
        if n == 4:
            psend(Z + 6, ref, lambda: zdev(-1))
        k1_push(n)

    def k1_forward(n):
        ref = lambda: (0, zz(zorder[n]), yy(-1))
        parrive(YL + n, ref)
        psend(YF + n, ref, lambda: ydev(1))

    own = lambda: (0, z, y)
    for n, d in ((3, 2), (4, -2), (1, 1), (2, -1)):
        psend(Z + n, own, lambda d=d: zdev(d))
    k1_push(0)

    for r in (4, 2, 3, 5, 6, 1, 7):
        hd = lax.rem(h + r, 8)
        go(
            lambda r=r, hd=hd: remote(
                kv_cols(hd), rows_of(TAIL + CH * h), k0s.at[r], k0r.at[h], (hd, c)
            )
        )
    row_h = [lax.rem(x * 2 + r, 8) for r in range(8)]

    def send_q(n, hd):
        go(lambda: remote(head_cols(q_ref, hd, 1024), qin.at[h], qs.at[n], qr.at[h], (hd, c)))

    send_q(4, row_h[4])
    send_q(5, row_h[5])

    def make_lists(s):
        rowv = par[s]
        flag = jnp.where(lane < 64, rowv, 0)
        rank = flag
        for step in (1, 2, 4, 8, 16, 32):
            rank = rank + jnp.where(lane >= step, pltpu.roll(rank, step, 1), 0)
        tab = jnp.where(lane >= 64, rowv, 0)
        for i in range(8):
            at = jnp.sum(jnp.where((flag == 1) & (rank == i + 1), lane, 0), axis=1, keepdims=True)
            tab = tab + jnp.where(lane == i, at, 0)
        tab = tab + jnp.where(lane == 8, jnp.sum(flag, axis=1, keepdims=True), 0)
        lst[s] = tab

    make_lists(0)

    @pl.loop(0, 8)
    def _(j):
        vg[j, :, 256:384] = jnp.ones((512, 128), jnp.bfloat16)

    k1_arrive(1)
    k1_arrive(2)
    k1_arrive(3)
    k1_arrive(4)
    k1_forward(0)
    to_smem = pltpu.make_async_copy(lst, lists, loc.at[1])
    to_smem.start()
    for r in range(1, 8):
        src = lax.rem(h + r, 8)
        arrived(rows_of(TAIL + CH * src), k0s.at[r], k0r.at[src])
    locals_[0].wait()
    go(
        lambda: remote(rows_of(TAIL + BLK, TAIL), rows_of(0, TAIL), ts.at[0], tr.at[0], (h, nxt)),
        lambda: c != 31,
    )
    go(
        lambda: remote(
            cache_ref.at[pl.ds(49, 15)], rows_of(0, TAIL), ts.at[0], tr.at[0], (h, nxt)
        ),
        lambda: c == 31,
    )

    for n in (2, 6, 3, 7):
        send_q(n, row_h[n])
    send_q(1, x * 2 + 1 - core)
    k1_forward(1)
    k1_forward(2)
    k1_arrive(5)
    k1_arrive(6)
    k1_arrive(7)
    k1_forward(3)
    k1_forward(4)
    k1_forward(5)
    k1_forward(6)
    k1_forward(7)
    for n in range(8):
        parrive(YS + n, lambda n=n: (0, zz(zorder[n]), yy(1)))
    for n in range(8):
        parrive(YF + n, lambda n=n: (0, zz(zorder[n]), yy(-2)))
    to_smem.wait()
    arrived(rows_of(0, TAIL), ts.at[0], tr.at[0])

    def gather(s):
        @pl.loop(0, 8)
        def _(j):
            for i in range(8):
                vg[j, pl.ds(i * BLK, BLK), 0:256] = pool0[jnp.clip(lists[s, j, i], 0, 63)]

    nt = (((1,), (1,)), ((), ()))
    f32, bf = jnp.float32, jnp.bfloat16

    def attend(p, s, first, j):
        cols = slice(j * W, (j + 1) * W)
        q = jnp.concatenate([qin[2 * p, :, cols], qin[2 * p + 1, :, cols]], axis=0)
        vlane = lax.broadcasted_iota(jnp.int32, (1, 512), 1)
        vbias = jnp.where(vlane < lists[s, j, 8] * BLK, 0.0, NEG)
        qrow = lax.broadcasted_iota(jnp.int32, (BLK, 256), 0)
        krow = lax.broadcasted_iota(jnp.int32, (BLK, 256), 1)
        keep = ((krow >= BLK) | (krow <= qrow)) & (krow < lists[s, j, 68] * BLK)
        sv = lax.dot_general(q, vg[j, :, :W], nt, preferred_element_type=f32)
        pvs, accs = [], []
        for b in range(4):
            keys = []
            for i in range(4):
                start = first + b
                if i:
                    start = start - jnp.clip(lists[s, j, 64 + i], 0, 15)
                keys.append(band0[start])
            ks = jnp.concatenate(keys, axis=0)
            part = slice(b * BLK, (b + 1) * BLK)
            ss = lax.dot_general(q[part], ks[:, :W], nt, preferred_element_type=f32)
            tv = sv[part] * COEF + vbias
            tsl = jnp.where(keep, ss * COEF, NEG)
            m = jnp.maximum(jnp.max(tv, axis=1, keepdims=True), jnp.max(tsl, axis=1, keepdims=True))
            pvs.append(jnp.exp2(tv - m).astype(bf))
            psl = jnp.exp2(tsl - m).astype(bf)
            vs = jnp.concatenate([ks[:, W:], jnp.ones((256, W), bf)], axis=1)
            accs.append(jnp.dot(psl, vs, preferred_element_type=f32))
        acc = jnp.dot(jnp.concatenate(pvs, axis=0), vg[j, :, W:], preferred_element_type=f32)
        acc += jnp.concatenate(accs, axis=0)
        o = (acc[:, :W] / acc[:, W:]).astype(bf)
        obuf[2 * p, :, cols] = o[:CH]
        obuf[2 * p + 1, :, cols] = o[CH:]

    def out_copy(dev, n, to, half):
        return remote(
            obuf.at[dev, :, 512 * half : 512 * half + 512],
            head_cols(out_ref, 2 * h + half, 512),
            os_.at[2 * n + half],
            or_.at[2 * h + half],
            (to, c),
        )

    own_out = pltpu.make_async_copy(obuf.at[h], head_cols(out_ref, h, 1024), loc.at[2])
    gather(0)
    chips = [lax.rem(x + r, 4) for r in range(4)]

    @pl.loop(0, 4)
    def _(t):
        for r in range(1, 4):

            @pl.when(t == ORDER.index(r))
            def _(r=r):
                for cc in range(2):
                    src = row_h[2 * r + cc]
                    arrived(qin.at[src], qs.at[1], qr.at[src])

        @pl.when(t == 3)
        def _():
            other = x * 2 + 1 - core
            arrived(qin.at[other], qs.at[1], qr.at[other])
            locals_[1].wait()

        p = jnp.where(t == 0, chips[ORDER[0]], jnp.where(t == 1, chips[ORDER[1]], jnp.where(t == 2, chips[ORDER[2]], x)))
        for half in range(2):
            for j in range(4 * half, 4 * half + 4):
                attend(p, 0, 15 + 4 * p, j)

            for r in range(1, 4):

                @pl.when(t == ORDER.index(r))
                def _(r=r, half=half):
                    for cc in range(2):
                        to = row_h[2 * r + cc]
                        out_copy(to, 2 * r + cc, to, half).start()

    other = x * 2 + 1 - core
    for half in range(2):
        out_copy(other, 1, other, half).start()
    own_out.start()
    own_out.wait()
    for r in range(1, 8):
        k = lax.rem(h + r, 8)
        for half in range(2):
            arrived(head_cols(out_ref, 2 * k + half, 512), os_.at[1], or_.at[2 * k + half])
    for half in range(2):
        for r in range(2, 8):
            out_copy(row_h[r], r, row_h[r], half).wait_send()
        out_copy(other, 1, other, half).wait_send()
    for make, cond in sent:
        if cond is None:
            make().wait_send()
        else:

            @pl.when(cond())
            def _(make=make):
                make().wait_send()


def finish(src, dst, sems):
    copies = [
        pltpu.make_async_copy(src.at[0, pl.ds(16 * i, 16)], dst.at[0, pl.ds(16 * i, 16)], sems.at[i])
        for i in range(8)
    ]
    for cp in copies:
        cp.start()
    for cp in copies:
        cp.wait()


def per_device(
    queries,
    segment_kv,
    cache_kv,
    vertical_ids,
    vertical_counts,
    vertical_heads,
    slash_offsets,
    slash_counts,
):
    bf = jnp.bfloat16
    dma = pltpu.SemaphoreType.DMA
    hbm = pl.BlockSpec(memory_space=pltpu.HBM)
    smem = pl.BlockSpec(memory_space=pltpu.SMEM)
    vmem = pl.BlockSpec(memory_space=pltpu.VMEM)
    shape = jax.ShapeDtypeStruct((1, CH, 8192), bf)
    result = pl.pallas_call(
        kernel,
        out_shape=shape,
        in_specs=[smem, smem, smem, smem, vmem, hbm, hbm, hbm],
        out_specs=vmem,
        scratch_shapes=[
            pltpu.VMEM((8, CH, 1024), bf),
            pltpu.VMEM((8, CH, 1024), bf),
            pltpu.VMEM((31, BLK, 256), bf),
            pltpu.VMEM((64, BLK, 256), bf),
            pltpu.VMEM((48, BLK, 256), bf),
            pltpu.VMEM((8, 512, 384), bf),
            pltpu.VMEM((1, 8, 128), jnp.int32),
            pltpu.VMEM((1, 8, 128), jnp.int32),
            pltpu.SMEM((1, 8, 128), jnp.int32),
            dma((6,)),
            dma((8,)),
            dma((8,)),
            dma((8,)),
            dma((8,)),
            dma((16,)),
            dma((16,)),
            dma((1,)),
            dma((1,)),
            dma((32,)),
            dma((32,)),
        ],
        compiler_params=pltpu.CompilerParams(
            collective_id=0, has_side_effects=True, vmem_limit_bytes=60 << 20
        ),
        cost_estimate=pl.CostEstimate(
            flops=2 * 2 * 8 * 1024 * 768 * W, bytes_accessed=8 << 20, transcendentals=8 * 1024 * 768
        ),
    )(
        vertical_ids,
        vertical_counts,
        slash_offsets.T,
        slash_counts.reshape(1, 8),
        vertical_heads,
        queries,
        segment_kv.reshape(2, BLK, 2048),
        cache_kv.reshape(64, BLK, 256),
    )
    return pl.pallas_call(
        finish,
        out_shape=shape,
        in_specs=[pl.BlockSpec(memory_space=pl.ANY)],
        out_specs=hbm,
        scratch_shapes=[dma((8,))],
        compiler_params=pltpu.CompilerParams(vmem_limit_bytes=8 << 20),
    )(result)


def solution(mesh):
    in_specs = (
        P("ctx", "head", None),
        P("ctx", "head", None),
        P("ctx", "head"),
        P("head", "ctx", None),
        P("head", None),
        P("head", None),
        P("head", None),
        P("head"),
    )
    return jax.shard_map(
        per_device,
        mesh=mesh,
        in_specs=in_specs,
        out_specs=P("ctx", "head", None),
        check_vma=False,
    )
```

```python
import functools
import math

import jax
import jax.numpy as jnp
from jax import lax
from jax.experimental import pallas as pl
from jax.experimental.pallas import tpu as pltpu
from jax.sharding import PartitionSpec as P

MESH = pl.DeviceIdType.MESH
W = 128
BLK = 64
CH = 128
TAIL = 960
NEG = -1e30
ORDER = (2, 1, 3)
COEF = W**-0.5 * math.log2(math.e)


def kernel(
    ids_ref,
    counts_ref,
    offs_ref,
    slash_ref,
    heads_ref,
    q_ref,
    kv_ref,
    cache_ref,
    out_ref,
    qin,
    obuf,
    band0,
    pool0,
    cachev,
    vg,
    par,
    lst,
    lists,
    loc,
    k0s,
    k0r,
    qs,
    qr,
    os_,
    or_,
    ts,
    tr,
    ps,
    pr,
):
    h = lax.axis_index("head")
    c = lax.axis_index("ctx")
    x, core = h // 2, lax.rem(h, 2)
    z, y = c // 4, lax.rem(c, 4)
    D = -1
    nxt = lax.rem(c + 1, 32)
    prv = lax.rem(c + 31, 32)

    zs = {s: lax.rem(z + s * D + 16, 8) for s in range(-4, 4)}
    ys = {s: lax.rem(y + s * D + 8, 4) for s in range(-2, 3)}
    def zz(s):
        return zs[s]

    def yy(s):
        return ys[s]

    def zdev(s):
        return (h, zz(s) * 4 + y)

    def ydev(s):
        return (h, z * 4 + yy(s))

    sent = []

    def go(make, cond=None):
        if cond is None:
            make().start()
        else:

            @pl.when(cond())
            def _():
                make().start()

        sent.append((make, cond))

    def remote(src, dst, ss, rs, dev):
        return pltpu.make_async_remote_copy(
            src_ref=src, dst_ref=dst, send_sem=ss, recv_sem=rs, device_id=dev, device_id_type=MESH
        )

    def arrived(dst, ss, rs):
        remote(dst, dst, ss, rs, (h, c)).wait_recv()

    def head_cols(ref, j, width):
        return ref.at[0, :, pl.ds(pl.multiple_of(j * width, width), width)]

    def kv_cols(j):
        return kv_ref.at[:, :, pl.ds(pl.multiple_of(j * 256, 256), 256)]

    def rows_of(start, size=CH):
        return band0.at[pl.ds(start // BLK, size // BLK)]

    load_cache = pltpu.make_async_copy(cache_ref.at[pl.ds(0, 48)], cachev, loc.at[0])
    load_cache.start()
    locals_ = [
        pltpu.make_async_copy(src, dst, loc.at[2 + i])
        for i, (src, dst) in enumerate(
            [
                (kv_cols(h), rows_of(TAIL + CH * h)),
                (head_cols(q_ref, h, 1024), qin.at[h]),
            ]
        )
    ]
    for cp in locals_:
        cp.start()

    barrier = pltpu.get_barrier_semaphore()

    def greet(dev):
        pl.semaphore_signal(barrier, inc=1, device_id=dev, device_id_type=MESH)

    for s in (-2, -1, 1, 2):
        greet(zdev(s))
    for s in (-1, 1):
        greet(ydev(s))

    greet((h, prv))
    for r in range(1, 8):
        greet((lax.rem(h + r, 8), c))

    lane = lax.broadcasted_iota(jnp.int32, (8, 128), 1)
    row = lax.broadcasted_iota(jnp.int32, (8, 128), 0)
    live = jnp.zeros((8, 128), jnp.int32)
    for i in range(32):
        live = jnp.where(lane // 2 == i, counts_ref[0, i], live)
    table = jnp.zeros((8, 128), jnp.int32)
    for j in range(8):
        for i in range(4):
            table = jnp.where((row == j) & (lane == 64 + i), offs_ref[i, j], table)
        table = jnp.where((row == j) & (lane == 68), slash_ref[0, j], table)
    par[0] = table
    par[0, :, 0:64] = jnp.where(lax.rem(lane, 2) < live, 1, 0)[:, 0:64] * heads_ref[...]

    pl.semaphore_wait(barrier, 14)

    def piece(k, zpos, ypos):
        return pool0.at[pl.ds((zpos * 4 + ypos) * 2 + k, 1)]

    load_cache.wait()
    for i in range(2):
        pool0[c * 2 + i] = cachev[ids_ref[0, 0, i]]

    def psend(n, place, to):
        go(lambda: remote(piece(*place()), piece(*place()), ps.at[n], pr.at[n], to()))

    def parrive(n, place):
        arrived(piece(*place()), ps.at[n], pr.at[n])

    Z, YL, YS, YF = 0, 8, 16, 24
    zorder = [0, -1, 1, -2, 2, -3, 3, -4]

    def k1_push(n):
        ref = lambda: (0, zz(zorder[n]), y)
        psend(YL + n, ref, lambda: ydev(1))
        psend(YS + n, ref, lambda: ydev(-1))

    def k1_arrive(n):
        ref = lambda: (0, zz(zorder[n]), y)
        parrive(Z + n, ref)
        if n == 3:
            psend(Z + 5, ref, lambda: zdev(1))
            psend(Z + 7, ref, lambda: zdev(2))
        if n == 4:
            psend(Z + 6, ref, lambda: zdev(-1))
        k1_push(n)

    def k1_forward(n):
        ref = lambda: (0, zz(zorder[n]), yy(-1))
        parrive(YL + n, ref)
        psend(YF + n, ref, lambda: ydev(1))

    BY, BZ = 32, 34
    yorder = [0, -1, 1, -2]

    def b_start(i):
        ref = lambda: (1, z, yy(yorder[i]))
        for m, d in ((3, 2), (4, -2), (1, 1), (2, -1)):
            psend(BZ + 7 * i + m, ref, lambda d=d: zdev(d))

    def b_arrive(i, m):
        ref = lambda: (1, zz(zorder[m]), yy(yorder[i]))
        parrive(BZ + 7 * i + m, ref)
        if m == 3:
            psend(BZ + 7 * i + 5, ref, lambda: zdev(1))
            psend(BZ + 7 * i + 7, ref, lambda: zdev(2))
        if m == 4:
            psend(BZ + 7 * i + 6, ref, lambda: zdev(-1))

    own = lambda: (0, z, y)
    psend(BY, lambda: (1, z, y), lambda: ydev(1))
    psend(BY + 1, lambda: (1, z, y), lambda: ydev(-1))
    b_start(0)
    for n, d in ((3, 2), (4, -2), (1, 1), (2, -1)):
        psend(Z + n, own, lambda d=d: zdev(d))
    k1_push(0)

    for r in (4, 2, 3, 5, 6, 1, 7):
        hd = lax.rem(h + r, 8)
        go(
            lambda r=r, hd=hd: remote(
                kv_cols(hd), rows_of(TAIL + CH * h), k0s.at[r], k0r.at[h], (hd, c)
            )
        )
    row_h = [lax.rem(x * 2 + r, 8) for r in range(8)]

    def send_q(n, hd):
        go(lambda: remote(head_cols(q_ref, hd, 1024), qin.at[h], qs.at[n], qr.at[h], (hd, c)))

    send_q(4, row_h[4])
    send_q(5, row_h[5])

    def make_lists(s):
        rowv = par[s]
        flag = jnp.where(lane < 64, rowv, 0)
        rank = flag
        for step in (1, 2, 4, 8, 16, 32):
            rank = rank + jnp.where(lane >= step, pltpu.roll(rank, step, 1), 0)
        tab = jnp.where(lane >= 64, rowv, 0)
        for i in range(8):
            at = jnp.sum(jnp.where((flag == 1) & (rank == i + 1), lane, 0), axis=1, keepdims=True)
            tab = tab + jnp.where(lane == i, at, 0)
        tab = tab + jnp.where(lane == 8, jnp.sum(flag, axis=1, keepdims=True), 0)
        lst[s] = tab

    make_lists(0)

    @pl.loop(0, 8)
    def _(j):
        vg[j, :, 256:384] = jnp.ones((512, 128), jnp.bfloat16)

    parrive(BY, lambda: (1, z, yy(-1)))
    psend(BY + 2, lambda: (1, z, yy(-1)), lambda: ydev(1))
    b_start(1)
    parrive(BY + 1, lambda: (1, z, yy(1)))
    b_start(2)
    k1_arrive(1)
    k1_arrive(2)
    k1_arrive(3)
    k1_arrive(4)
    k1_forward(0)
    to_smem = pltpu.make_async_copy(lst, lists, loc.at[1])
    to_smem.start()
    for r in range(1, 8):
        src = lax.rem(h + r, 8)
        arrived(rows_of(TAIL + CH * src), k0s.at[r], k0r.at[src])
    locals_[0].wait()
    go(
        lambda: remote(rows_of(TAIL + BLK, TAIL), rows_of(0, TAIL), ts.at[0], tr.at[0], (h, nxt)),
        lambda: c != 31,
    )
    go(
        lambda: remote(
            cache_ref.at[pl.ds(49, 15)], rows_of(0, TAIL), ts.at[0], tr.at[0], (h, nxt)
        ),
        lambda: c == 31,
    )

    for n in (2, 6, 3, 7):
        send_q(n, row_h[n])
    send_q(1, x * 2 + 1 - core)
    parrive(BY + 2, lambda: (1, z, yy(-2)))
    b_start(3)
    k1_forward(1)
    k1_forward(2)
    for i in range(3):
        b_arrive(i, 3)
        b_arrive(i, 4)
    k1_arrive(5)
    k1_arrive(6)
    k1_arrive(7)
    k1_forward(3)
    k1_forward(4)
    k1_forward(5)
    k1_forward(6)
    k1_forward(7)
    b_arrive(3, 3)
    b_arrive(3, 4)
    for i in range(4):
        for m in (1, 2, 5, 6, 7):
            b_arrive(i, m)
    for n in range(8):
        parrive(YS + n, lambda n=n: (0, zz(zorder[n]), yy(1)))
    for n in range(8):
        parrive(YF + n, lambda n=n: (0, zz(zorder[n]), yy(-2)))
    to_smem.wait()
    arrived(rows_of(0, TAIL), ts.at[0], tr.at[0])

    def gather(s):
        @pl.loop(0, 8)
        def _(j):
            for i in range(8):
                vg[j, pl.ds(i * BLK, BLK), 0:256] = pool0[jnp.clip(lists[s, j, i], 0, 63)]

    nt = (((1,), (1,)), ((), ()))
    f32, bf = jnp.float32, jnp.bfloat16

    def attend(p, s, first, j):
        cols = slice(j * W, (j + 1) * W)
        q = jnp.concatenate([qin[2 * p, :, cols], qin[2 * p + 1, :, cols]], axis=0)
        vlane = lax.broadcasted_iota(jnp.int32, (1, 512), 1)
        vbias = jnp.where(vlane < lists[s, j, 8] * BLK, 0.0, NEG)
        qrow = lax.broadcasted_iota(jnp.int32, (BLK, 256), 0)
        krow = lax.broadcasted_iota(jnp.int32, (BLK, 256), 1)
        keep = ((krow >= BLK) | (krow <= qrow)) & (krow < lists[s, j, 68] * BLK)
        sv = lax.dot_general(q, vg[j, :, :W], nt, preferred_element_type=f32)
        pvs, accs = [], []
        for b in range(4):
            keys = []
            for i in range(4):
                start = first + b
                if i:
                    start = start - jnp.clip(lists[s, j, 64 + i], 0, 15)
                keys.append(band0[start])
            ks = jnp.concatenate(keys, axis=0)
            part = slice(b * BLK, (b + 1) * BLK)
            ss = lax.dot_general(q[part], ks[:, :W], nt, preferred_element_type=f32)
            tv = sv[part] * COEF + vbias
            tsl = jnp.where(keep, ss * COEF, NEG)
            m = jnp.maximum(jnp.max(tv, axis=1, keepdims=True), jnp.max(tsl, axis=1, keepdims=True))
            pvs.append(jnp.exp2(tv - m).astype(bf))
            psl = jnp.exp2(tsl - m).astype(bf)
            vs = jnp.concatenate([ks[:, W:], jnp.ones((256, W), bf)], axis=1)
            accs.append(jnp.dot(psl, vs, preferred_element_type=f32))
        acc = jnp.dot(jnp.concatenate(pvs, axis=0), vg[j, :, W:], preferred_element_type=f32)
        acc += jnp.concatenate(accs, axis=0)
        o = (acc[:, :W] / acc[:, W:]).astype(bf)
        obuf[2 * p, :, cols] = o[:CH]
        obuf[2 * p + 1, :, cols] = o[CH:]

    def out_copy(dev, n, to, half):
        return remote(
            obuf.at[dev, :, 512 * half : 512 * half + 512],
            head_cols(out_ref, 2 * h + half, 512),
            os_.at[2 * n + half],
            or_.at[2 * h + half],
            (to, c),
        )

    own_out = pltpu.make_async_copy(obuf.at[h], head_cols(out_ref, h, 1024), loc.at[2])
    gather(0)
    chips = [lax.rem(x + r, 4) for r in range(4)]

    @pl.loop(0, 4)
    def _(t):
        for r in range(1, 4):

            @pl.when(t == ORDER.index(r))
            def _(r=r):
                for cc in range(2):
                    src = row_h[2 * r + cc]
                    arrived(qin.at[src], qs.at[1], qr.at[src])

        @pl.when(t == 3)
        def _():
            other = x * 2 + 1 - core
            arrived(qin.at[other], qs.at[1], qr.at[other])
            locals_[1].wait()

        p = jnp.where(t == 0, chips[ORDER[0]], jnp.where(t == 1, chips[ORDER[1]], jnp.where(t == 2, chips[ORDER[2]], x)))
        for half in range(2):
            for j in range(4 * half, 4 * half + 4):
                attend(p, 0, 15 + 4 * p, j)

            for r in range(1, 4):

                @pl.when(t == ORDER.index(r))
                def _(r=r, half=half):
                    for cc in range(2):
                        to = row_h[2 * r + cc]
                        out_copy(to, 2 * r + cc, to, half).start()

    other = x * 2 + 1 - core
    for half in range(2):
        out_copy(other, 1, other, half).start()
    own_out.start()
    own_out.wait()
    for r in range(1, 8):
        k = lax.rem(h + r, 8)
        for half in range(2):
            arrived(head_cols(out_ref, 2 * k + half, 512), os_.at[1], or_.at[2 * k + half])
    for half in range(2):
        for r in range(2, 8):
            out_copy(row_h[r], r, row_h[r], half).wait_send()
        out_copy(other, 1, other, half).wait_send()
    for make, cond in sent:
        if cond is None:
            make().wait_send()
        else:

            @pl.when(cond())
            def _(make=make):
                make().wait_send()


def finish(src, dst, sems):
    copies = [
        pltpu.make_async_copy(src.at[0, pl.ds(16 * i, 16)], dst.at[0, pl.ds(16 * i, 16)], sems.at[i])
        for i in range(8)
    ]
    for cp in copies:
        cp.start()
    for cp in copies:
        cp.wait()


def per_device(
    queries,
    segment_kv,
    cache_kv,
    vertical_ids,
    vertical_counts,
    vertical_heads,
    slash_offsets,
    slash_counts,
):
    bf = jnp.bfloat16
    dma = pltpu.SemaphoreType.DMA
    hbm = pl.BlockSpec(memory_space=pltpu.HBM)
    smem = pl.BlockSpec(memory_space=pltpu.SMEM)
    vmem = pl.BlockSpec(memory_space=pltpu.VMEM)
    shape = jax.ShapeDtypeStruct((1, CH, 8192), bf)
    result = pl.pallas_call(
        kernel,
        out_shape=shape,
        in_specs=[smem, smem, smem, smem, vmem, hbm, hbm, hbm],
        out_specs=vmem,
        scratch_shapes=[
            pltpu.VMEM((8, CH, 1024), bf),
            pltpu.VMEM((8, CH, 1024), bf),
            pltpu.VMEM((31, BLK, 256), bf),
            pltpu.VMEM((64, BLK, 256), bf),
            pltpu.VMEM((48, BLK, 256), bf),
            pltpu.VMEM((8, 512, 384), bf),
            pltpu.VMEM((1, 8, 128), jnp.int32),
            pltpu.VMEM((1, 8, 128), jnp.int32),
            pltpu.SMEM((1, 8, 128), jnp.int32),
            dma((6,)),
            dma((8,)),
            dma((8,)),
            dma((8,)),
            dma((8,)),
            dma((16,)),
            dma((16,)),
            dma((1,)),
            dma((1,)),
            dma((63,)),
            dma((63,)),
        ],
        compiler_params=pltpu.CompilerParams(
            collective_id=0, has_side_effects=True, vmem_limit_bytes=60 << 20
        ),
        cost_estimate=pl.CostEstimate(
            flops=2 * 2 * 8 * 1024 * 768 * W, bytes_accessed=8 << 20, transcendentals=8 * 1024 * 768
        ),
    )(
        vertical_ids,
        vertical_counts,
        slash_offsets.T,
        slash_counts.reshape(1, 8),
        vertical_heads,
        queries,
        segment_kv.reshape(2, BLK, 2048),
        cache_kv.reshape(64, BLK, 256),
    )
    return pl.pallas_call(
        finish,
        out_shape=shape,
        in_specs=[pl.BlockSpec(memory_space=pl.ANY)],
        out_specs=hbm,
        scratch_shapes=[dma((8,))],
        compiler_params=pltpu.CompilerParams(vmem_limit_bytes=8 << 20),
    )(result)


def solution(mesh):
    in_specs = (
        P("ctx", "head", None),
        P("ctx", "head", None),
        P("ctx", "head"),
        P("head", "ctx", None),
        P("head", None),
        P("head", None),
        P("head", None),
        P("head"),
    )
    return jax.shard_map(
        per_device,
        mesh=mesh,
        in_specs=in_specs,
        out_specs=P("ctx", "head", None),
        check_vma=False,
    )
```
